768 devices in a mesh: leaf: 384 (over x, z, y), grp: 2 (over core).
Axes of the slice: x: 4, y: 8, z: 12, core: 2. Of those that a mesh axis runs over, the one named last changes fastest.
Arguments:
- charges: bfloat16 [1536, 8, 256], P(('leaf', 'grp')), may hold values from -6 to 6
- leaf_basis: bfloat16 [1536, 64, 256], P(('leaf', 'grp')), may hold values from -0.375 to 0.375
- transfers: float32 [768, 3, 64, 64], P(('leaf', 'grp')), may hold values from -0.75 to 0.75
- near_blocks: bfloat16 [1536, 6, 256, 256], P(('leaf', 'grp')), may hold values from -0.15625 to 0.15625
- near_list: int32 [1536, 6], P(('leaf', 'grp')), may hold values from 0 to 1535, as said below
- near_count: int32 [1536], P(('leaf', 'grp')), may hold values from 1 to 6, as said below
- dev_coupling: float32 [768, 8, 64, 64], P(('leaf', 'grp')), may hold values from -0.25 to 0.25
- dev_list: int32 [768, 8], P(('leaf', 'grp')), may hold values from 0 to 767, as said below
- dev_count: int32 [768], P(('leaf', 'grp')), may hold values from 1 to 8, as said below
- pair_coupling: float32 [384, 16, 64, 64], P('leaf', 'grp'), may hold values from -0.1875 to 0.1875
- pair_list: int32 [384, 16], P('leaf', 'grp'), may hold values from 0 to 383, as said below
- pair_count: int32 [384], P('leaf'), may hold values from 1 to 16, as said below
Outputs:
- potentials: float32 [1536, 8, 256], P(('leaf', 'grp'))
The draws below stay inside these ranges and needn't reach their ends.
Inputs may be any that keep to these rules, and one draw needn't show every extreme that they name: `near_list`: row i names leaves at most 2 places from i; slot 0 is i itself. `near_count`: slots from the count on are unused; some leaf uses all of them. `dev_list`: names subtrees 1 to 5 places from the subtree itself or 768 // 2 places on, counted cyclically; some row names a subtree 5 places on, some row one 5 places back, and some row one half the subtrees on. `dev_count`: slots from the count on are unused; some subtree uses all of them. `pair_list`: names pairs 1 to 5 places from the pair itself or 384 // 2 places on, counted cyclically; some row names a pair 5 places on, some row one 5 places back, and some row one half the pairs on. `pair_count`: slots from the count on are unused; some pair uses all of them.
All inputs are finite; a program needn't handle non-finite values.
Results may differ from the reference program's by a relative error of at most 0.0004.
Values may be sent and summed in bfloat16 or wider, within the bound.
A program may use at most 32 MiB of HBM per device.

```python
import jax
import jax.numpy as jnp
from jax import lax

P_SIZE = 256
K = 64
R = 8
NEAR = 6
NFAR = 8
LEAF_DEV = 2
CLUSTERS = 768
PAIRS = 384
LEAVES = 1536
TRN = 3


def forced_counts(key, total_rows, largest):
    count_key, place_key = jax.random.split(key)
    counts = jax.random.randint(count_key, (total_rows,), 1, largest + 1)
    where_full = jax.random.randint(place_key, (), 0, total_rows)
    return counts.at[where_full].set(largest).astype(jnp.int32)


def cyclic_far(key, total_rows, slots):
    size_key, sign_key, half_key = jax.random.split(key, 3)
    magnitude = jax.random.randint(size_key, (total_rows, slots), 1, 6)
    signs = jax.random.randint(sign_key, (total_rows, slots), 0, 2) * 2 - 1
    steps = magnitude * signs
    far_pick = jax.random.randint(half_key, (total_rows, slots), 0, 8)
    steps = jnp.where(far_pick == 0, total_rows // 2, steps)
    steps = steps.at[0, 0].set(5)
    steps = steps.at[1, 0].set(-5)
    steps = steps.at[2, 0].set(-1)
    steps = steps.at[3, 0].set(total_rows // 2)
    rows = jnp.arange(total_rows, dtype=jnp.int32)[:, None]
    return ((rows + steps) % total_rows).astype(jnp.int32)


def draw_near_count(key, part):
    key = jax.random.fold_in(key, 11)
    return forced_counts(key, LEAVES, NEAR)


def draw_dev_count(key, part):
    key = jax.random.fold_in(key, 12)
    return forced_counts(key, CLUSTERS, NFAR)


def draw_pair_count(key, part):
    key = jax.random.fold_in(key, 13)
    return forced_counts(key, PAIRS, 2 * NFAR)


def draw_near_list(key, part):
    key = jax.random.fold_in(key, 14)
    offsets = jax.random.randint(key, (LEAVES, NEAR), -LEAF_DEV, LEAF_DEV + 1)
    offsets = offsets.at[:, 0].set(0)
    rows = jnp.arange(LEAVES, dtype=jnp.int32)[:, None]
    return jnp.clip(rows + offsets, 0, LEAVES - 1).astype(jnp.int32)


def draw_dev_list(key, part):
    key = jax.random.fold_in(key, 15)
    return cyclic_far(key, CLUSTERS, NFAR)


def draw_pair_list(key, part):
    key = jax.random.fold_in(key, 16)
    return cyclic_far(key, PAIRS, 2 * NFAR)


def block_levels(rng, extent, cuts, low, top_value):
    def one(axis_at, blocks):
        heights = jax.random.uniform(jax.random.fold_in(jax.random.fold_in(rng, 6), axis_at), (blocks,), jnp.float32, low / len(cuts), top_value / len(cuts))
        return jnp.repeat(jnp.exp(heights), extent[axis_at] // blocks).reshape((-1,) + (1,) * (len(extent) - axis_at - 1))

    factor_of = one(*cuts[0])
    for cut in cuts[1:]:
        factor_of = factor_of * one(*cut)
    return factor_of


def gaussian(own_key, shape, width, limit, cuts=(), held_as=jnp.bfloat16):
    loudness = block_levels(own_key, shape, cuts, -0.22, 0.18) if cuts else 1.0
    result = jax.random.normal(own_key, shape, jnp.float32) * width * loudness
    return jnp.minimum(jnp.maximum(result, -limit), limit).astype(held_as)


def setup_inputs(seed: int = 0) -> dict:
    splits = jax.random.split(jax.random.key(seed), 13)
    return {
        "charges": gaussian(splits[0], (LEAVES, R, P_SIZE), 1.0, 6.0, ((0, 768),)),
        "leaf_basis": gaussian(splits[1], (LEAVES, K, P_SIZE), P_SIZE ** -0.5, 0.375, ((0, 768),)),
        "transfers": gaussian(splits[2], (CLUSTERS, TRN, K, K), K ** -0.5, 0.75, ((0, 768),), jnp.float32),
        "near_blocks": gaussian(splits[3], (LEAVES, NEAR, P_SIZE, P_SIZE), (P_SIZE * NEAR) ** -0.5, 0.15625, ((0, 768),)),
        "near_list": draw_near_list(jax.random.fold_in(splits[12], 71), 0),
        "near_count": draw_near_count(jax.random.fold_in(splits[12], 71), 0),
        "dev_coupling": gaussian(splits[6], (CLUSTERS, NFAR, K, K), (K * NFAR) ** -0.5, 0.25, ((0, 768),), jnp.float32),
        "dev_list": draw_dev_list(jax.random.fold_in(splits[12], 71), 0),
        "dev_count": draw_dev_count(jax.random.fold_in(splits[12], 71), 0),
        "pair_coupling": gaussian(splits[9], (PAIRS, 2 * NFAR, K, K), (2 * K * NFAR) ** -0.5, 0.1875, ((0, 384), (1, 2)), jnp.float32),
        "pair_list": draw_pair_list(jax.random.fold_in(splits[12], 71), 0),
        "pair_count": draw_pair_count(jax.random.fold_in(splits[12], 71), 0),
    }


def reference(charges, leaf_basis, transfers, near_blocks, near_list, near_count, dev_coupling, dev_list, dev_count, pair_coupling, pair_list, pair_count):
    exact_mode = lax.Precision.HIGHEST
    charge_float = charges.astype(jnp.float32)
    basis_float = leaf_basis.astype(jnp.float32)
    leaf_coeff = jnp.einsum("lrp,lkp->lrk", charge_float, basis_float, precision=exact_mode)
    section_coeff = leaf_coeff.reshape(CLUSTERS, LEAF_DEV, R, K)
    offset = 0
    members = LEAF_DEV
    sections = []
    while members > 1:
        matrices = transfers[:, offset:offset + members]
        lifted_section = jnp.einsum("dnrk,dnkj->dnrj", section_coeff, matrices, precision=exact_mode)
        section_coeff = lifted_section.reshape(CLUSTERS, members // 2, 2, R, K).sum(axis=2)
        sections.append((offset, members))
        offset = offset + members
        members = members // 2
    dev_coeff = section_coeff[:, 0]
    last_transfer = transfers[:, TRN - 1]
    lifted = jnp.einsum("drk,dkj->drj", dev_coeff, last_transfer, precision=exact_mode)
    pair_coeff = lifted.reshape(PAIRS, 2, R, K).sum(axis=1)
    dev_mask = (jnp.arange(NFAR)[None, :] < dev_count[:, None]).astype(jnp.float32)
    dev_sources = dev_coeff[dev_list] * dev_mask[:, :, None, None]
    dev_field = jnp.einsum("dsrk,dskj->drj", dev_sources, dev_coupling, precision=exact_mode)
    pair_mask = (jnp.arange(2 * NFAR)[None, :] < pair_count[:, None]).astype(jnp.float32)
    pair_sources = pair_coeff[pair_list] * pair_mask[:, :, None, None]
    pair_field = jnp.einsum("qsrk,qskj->qrj", pair_sources, pair_coupling, precision=exact_mode)
    pair_spread = jnp.repeat(pair_field, 2, axis=0)
    root_field = dev_field + jnp.einsum("drj,dkj->drk", pair_spread, last_transfer, precision=exact_mode)
    section_field = root_field[:, None]
    for offset, members in reversed(sections):
        spread = jnp.repeat(section_field, 2, axis=1)
        section_field = jnp.einsum("dnrj,dnkj->dnrk", spread, transfers[:, offset:offset + members], precision=exact_mode)
    leaf_field = section_field.reshape(LEAVES, R, K)
    far_part = jnp.einsum("lrk,lkp->lrp", leaf_field, basis_float, precision=exact_mode)

    def near_group(item):
        blocks, indices, counts = item
        picked = charges[indices].astype(jnp.float32)
        used = jnp.arange(NEAR)[None, :] < counts[:, None]
        picked = jnp.where(used[:, :, None, None], picked, jnp.zeros_like(picked))
        return jnp.einsum("lsrp,lspq->lrq", picked, blocks.astype(jnp.float32), precision=exact_mode)

    near_part = lax.map(near_group, (near_blocks.reshape(CLUSTERS, LEAF_DEV, NEAR, P_SIZE, P_SIZE), near_list.reshape(CLUSTERS, LEAF_DEV, NEAR), near_count.reshape(CLUSTERS, LEAF_DEV)))
    return near_part.reshape(LEAVES, R, P_SIZE) + far_part
```

```python
import functools

import jax
import jax.numpy as jnp
from jax import lax
from jax.experimental import pallas as pl
from jax.experimental.pallas import tpu as pltpu
from jax.sharding import PartitionSpec as P

MESH = pl.DeviceIdType.MESH
REACH = 5
F32 = jnp.float32
BF16 = jnp.bfloat16
NN = (((1,), (0,)), ((), ()))
NT = (((1,), (1,)), ((), ()))
TN = (((0,), (0,)), ((), ()))


def dot(a, b, dims=NN):
    return lax.dot_general(a, b, dims, preferred_element_type=F32)


def halves(a):
    high = a.astype(BF16)
    return high, (a - high.astype(F32)).astype(BF16)


def dot3(a, b, dims=NN):
    ah, al = halves(a)
    bh, bl = halves(b)
    return dot(ah, bh, dims) + dot(al, bh, dims) + dot(ah, bl, dims)


def stacked(a):
    high = a.astype(BF16).astype(F32)
    return jnp.concatenate([high, a - high], axis=0).astype(BF16)


def folded(a):
    return a[0:8] + a[8:16]


def kernel(
    pairs,
    charges,
    basis,
    transfers,
    near_blocks,
    near_list,
    near_count,
    dev_coupling,
    dev_list,
    dev_count,
    pair_coupling,
    pair_list,
    pair_count,
    out,
    charge_buf,
    basis_buf,
    transfer_buf,
    block_buf,
    dev_buf,
    pair_buf,
    tiles,
    w_high,
    w_low,
    s_near_list,
    s_near_count,
    s_dev_list,
    s_dev_count,
    s_pair_list,
    s_pair_count,
    partner_list,
    in_sem,
    tile_send,
    tile_recv,
    charge_send,
    charge_recv,
    coupling_send,
    coupling_recv,
    list_send,
    list_recv,
):
    q = lax.axis_index("leaf")
    g = lax.axis_index("grp")
    other = 1 - g
    half = pairs // 2
    own = REACH
    last = 2 * REACH + 1

    peers = [((q, other), 2 * own + g)]
    for shift in (half, 5, -5, 4, -4, 3, -3, 2, -2, 1, -1):
        there = lax.rem(q + (shift + pairs), pairs)
        place = last if shift == half else own - shift
        for core in (g, other):
            peers.append(((there, core), 2 * place + g))
    count = len(peers)

    local = [
        (charges, charge_buf.at[1]),
        (basis, basis_buf),
        (transfers, transfer_buf),
        (pair_coupling, pair_buf.at[0]),
        (dev_coupling, dev_buf),
        (near_blocks.at[0], block_buf.at[0]),
        (near_blocks.at[1], block_buf.at[1]),
        (near_list, s_near_list),
        (near_count, s_near_count),
        (dev_list, s_dev_list),
        (dev_count, s_dev_count),
        (pair_list, s_pair_list),
        (pair_count, s_pair_count),
    ]
    local = [pltpu.make_async_copy(a, b, in_sem.at[i]) for i, (a, b) in enumerate(local)]
    for copy in local[:3]:
        copy.start()
    barrier = pltpu.get_barrier_semaphore()
    for device, _ in peers:
        pl.semaphore_signal(barrier, inc=1, device_id=device, device_id_type=MESH)
    for copy in local[3:]:
        copy.start()

    for copy in local[:3]:
        copy.wait()
    e = transfer_buf[0]
    e01 = e[0:2].reshape(128, 64)
    up = jnp.concatenate([e01, dot3(e01, e[2])], axis=1)
    own_charges = charge_buf[1].astype(F32).reshape(16, 256).astype(BF16)
    cross = dot(own_charges, basis_buf[...].reshape(128, 256), NT)
    lane = lax.broadcasted_iota(jnp.int32, (8, 128), 1)
    leaf_coeff = stacked(jnp.where(lane < 64, cross[0:8], cross[8:16]))
    up_high, up_low = halves(up)
    my_tile = 2 * own + g
    tiles[my_tile] = folded(dot(leaf_coeff, up_high) + dot(leaf_coeff, up_low))

    pl.semaphore_wait(barrier, count)
    sends = []
    for device, place in peers:
        sends.append(
            pltpu.make_async_remote_copy(
                src_ref=tiles.at[my_tile],
                dst_ref=tiles.at[place],
                send_sem=tile_send,
                recv_sem=tile_recv,
                device_id=device,
                device_id_type=MESH,
            )
        )
    step = 2 * g - 1
    beside = (lax.rem(q + step + pairs, pairs), other)
    to_partner = pltpu.make_async_remote_copy(
        src_ref=charges,
        dst_ref=charge_buf.at[2 * g],
        send_sem=charge_send.at[0],
        recv_sem=charge_recv.at[0],
        device_id=(q, other),
        device_id_type=MESH,
    )
    to_beside = pltpu.make_async_remote_copy(
        src_ref=charges,
        dst_ref=charge_buf.at[2 - 2 * g],
        send_sem=charge_send.at[1],
        recv_sem=charge_recv.at[1],
        device_id=beside,
        device_id_type=MESH,
    )
    give_list = pltpu.make_async_remote_copy(
        src_ref=pair_list,
        dst_ref=partner_list,
        send_sem=list_send,
        recv_sem=list_recv,
        device_id=(q, other),
        device_id_type=MESH,
    )
    give_coupling = pltpu.make_async_remote_copy(
        src_ref=pair_coupling,
        dst_ref=pair_buf.at[1],
        send_sem=coupling_send,
        recv_sem=coupling_recv,
        device_id=(q, other),
        device_id_type=MESH,
    )
    others = [to_beside, to_partner, give_coupling, give_list]
    for copy in sends + others:
        copy.start()

    for copy in local[3:5]:
        copy.wait()
    for copy in local[7:]:
        copy.wait()
    e2h, e2l = halves(e[2])

    def through_pair(blocks):
        rows = blocks.reshape(512, 64)
        rh, rl = halves(rows)
        return (dot(rh, e2h, NT) + dot(rl, e2h, NT) + dot(rh, e2l, NT)).reshape(8, 64, 64)

    def used(slot, total):
        return jnp.where(slot < total, 1.0, 0.0).astype(F32)

    dev_total = s_dev_count[0]
    pair_total = s_pair_count[0]
    lifted = through_pair(pair_buf[0, 0])
    for s in range(8):
        w = jnp.concatenate(
            [dev_buf[0, s] * used(s, dev_total), lifted[s] * used(8 * g + s, pair_total)], axis=0
        )
        w_high[s], w_low[s] = halves(w)

    down = [
        dot(e_part, basis_buf[l], TN)
        for l in range(2)
        for e_part in halves(e[l])
    ]
    down = jnp.concatenate([down[0] + down[1], down[2] + down[3]], axis=1)
    down_high, down_low = halves(down)

    for copy in (to_beside, to_partner):
        copy.wait_recv()
    for copy in local[5:7]:
        copy.wait()
    first = 2 * (2 * q + g) - 2
    near = []
    for l in range(2):
        total = jnp.zeros((8, 256), F32)
        for s in range(6):
            at = jnp.clip(s_near_list[l, s] - first, 0, 5)
            picked = charge_buf[at // 2, at % 2].astype(F32) * used(s, s_near_count[l])
            total += dot(picked.astype(BF16), block_buf[l, s])
        near.append(total)

    give_coupling.wait_recv()
    give_list.wait_recv()
    lifted = through_pair(pair_buf[1, 0])
    for t in range(4):
        w = jnp.concatenate(
            [lifted[s] * used(8 * other + s, pair_total) for s in (2 * t, 2 * t + 1)], axis=0
        )
        w_high[8 + t], w_low[8 + t] = halves(w)

    def place_of(offset, rows):
        near_by = jnp.where(offset <= REACH, offset + REACH, offset - rows + REACH)
        return jnp.clip(jnp.where(offset == half, last, near_by), 0, last)

    dev_at, pair_at, partner_at = [], [], []
    for s in range(8):
        source = s_dev_list[0, s]
        offset = lax.rem(source // 2 - q + pairs, pairs)
        dev_at.append(2 * place_of(offset, pairs) + source % 2)
        pair_at.append(place_of(lax.rem(s_pair_list[0, s] - q + pairs, pairs), pairs))
        partner_at.append(place_of(lax.rem(partner_list[0, s] - q + pairs, pairs), pairs))

    everyone = tiles.at[pl.ds(0, count)]
    pltpu.make_async_copy(everyone, everyone, tile_recv).wait()
    root = jnp.zeros((16, 64), F32)

    def pair_tile(at):
        return tiles[2 * at] + tiles[2 * at + 1]

    for s in range(8):
        x = stacked(jnp.where(lane < 64, tiles[dev_at[s]], pair_tile(pair_at[s])))
        root += dot(x, w_high[s]) + dot(x, w_low[s])
    for t in range(4):
        low = pltpu.roll(pair_tile(partner_at[2 * t]), 64, 1)
        x = stacked(jnp.where(lane < 64, low, pair_tile(partner_at[2 * t + 1])))
        root += dot(x, w_high[8 + t]) + dot(x, w_low[8 + t])
    root = stacked(folded(root))
    far = folded(dot(root, down_high) + dot(root, down_low))
    for l in range(2):
        out[l] = near[l] + far[:, 256 * l : 256 * (l + 1)]

    pltpu.make_async_copy(everyone, everyone, tile_send).wait()
    for copy in others:
        copy.wait_send()


def per_device(*arrays):
    pairs = lax.axis_size("leaf")
    hbm = pl.BlockSpec(memory_space=pl.ANY)
    dma = pltpu.SemaphoreType.DMA
    return pl.pallas_call(
        functools.partial(kernel, pairs),
        out_shape=jax.ShapeDtypeStruct((2, 8, 256), F32),
        in_specs=[hbm] * len(arrays),
        out_specs=pl.BlockSpec(memory_space=pltpu.VMEM),
        scratch_shapes=[
            pltpu.VMEM((3, 2, 8, 256), BF16),
            pltpu.VMEM((2, 64, 256), BF16),
            pltpu.VMEM((1, 3, 64, 64), F32),
            pltpu.VMEM((2, 6, 256, 256), BF16),
            pltpu.VMEM((1, 8, 64, 64), F32),
            pltpu.VMEM((2, 1, 8, 64, 64), F32),
            pltpu.VMEM((24, 8, 128), F32),
            pltpu.VMEM((12, 128, 64), BF16),
            pltpu.VMEM((12, 128, 64), BF16),
            pltpu.SMEM((2, 6), jnp.int32),
            pltpu.SMEM((2,), jnp.int32),
            pltpu.SMEM((1, 8), jnp.int32),
            pltpu.SMEM((1,), jnp.int32),
            pltpu.SMEM((1, 8), jnp.int32),
            pltpu.SMEM((1,), jnp.int32),
            pltpu.SMEM((1, 8), jnp.int32),
            dma((13,)),
            dma,
            dma,
            dma((2,)),
            dma((2,)),
            dma,
            dma,
            dma,
            dma,
        ],
        compiler_params=pltpu.CompilerParams(
            collective_id=0, has_side_effects=True, vmem_limit_bytes=48 * 1024 * 1024
        ),
        name="h2_product",
    )(*arrays)


def solution(mesh):
    both = ("leaf", "grp")
    return jax.shard_map(
        per_device,
        mesh=mesh,
        in_specs=(
            P(both, None, None),
            P(both, None, None),
            P(both, None, None, None),
            P(both, None, None, None),
            P(both, None),
            P(both),
            P(both, None, None, None),
            P(both, None),
            P(both),
            P("leaf", "grp", None, None),
            P("leaf", "grp"),
            P("leaf"),
        ),
        out_specs=P(both, None, None),
        check_vma=False,
    )
```

```python
import functools

import jax
import jax.numpy as jnp
from jax import lax
from jax.experimental import pallas as pl
from jax.experimental.pallas import tpu as pltpu
from jax.sharding import PartitionSpec as P

MESH = pl.DeviceIdType.MESH
REACH = 5
F32 = jnp.float32
BF16 = jnp.bfloat16
NN = (((1,), (0,)), ((), ()))
NT = (((1,), (1,)), ((), ()))
TN = (((0,), (0,)), ((), ()))


def dot(a, b, dims=NN):
    return lax.dot_general(a, b, dims, preferred_element_type=F32)


def halves(a):
    high = a.astype(BF16)
    return high, (a - high.astype(F32)).astype(BF16)


def dot3(a, b, dims=NN):
    ah, al = halves(a)
    bh, bl = halves(b)
    return dot(ah, bh, dims) + dot(al, bh, dims) + dot(ah, bl, dims)


def stacked(a):
    high = a.astype(BF16).astype(F32)
    return jnp.concatenate([high, a - high], axis=0).astype(BF16)


def folded(a):
    return a[0:8] + a[8:16]


def kernel(
    pairs,
    charges,
    basis,
    transfers,
    near_blocks,
    near_list,
    near_count,
    dev_coupling,
    dev_list,
    dev_count,
    pair_coupling,
    pair_list,
    pair_count,
    out,
    charge_buf,
    basis_buf,
    transfer_buf,
    block_buf,
    dev_buf,
    pair_buf,
    tiles,
    weights,
    s_near_list,
    s_near_count,
    s_dev_list,
    s_dev_count,
    s_pair_list,
    s_pair_count,
    partner_list,
    in_sem,
    tile_send,
    tile_recv,
    charge_send,
    charge_recv,
    coupling_send,
    coupling_recv,
    list_send,
    list_recv,
):
    q = lax.axis_index("leaf")
    g = lax.axis_index("grp")
    other = 1 - g
    half = pairs // 2
    own = REACH
    last = 2 * REACH + 1

    peers = [(q, other, 2 * own + g, True)]
    side = 2 * g - 1
    for shift, same, cross in (
        (half, True, False),
        (5, False, False),
        (-5, False, False),
        (4, False, False),
        (-4, False, False),
        (3 * side, False, True),
        (-3 * side, False, False),
        (2, True, True),
        (-2, True, True),
        (1, True, True),
        (-1, True, True),
    ):
        there = lax.rem(q + (shift + pairs), pairs)
        place = 2 * (last if shift is half else own - shift) + g
        peers.append((there, g, place, same))
        peers.append((there, other, place, cross))
    count = len(peers)
    whole_tiles = sum(whole for *_, whole in peers)
    received = whole_tiles + (count - whole_tiles) // 2

    local = [
        (charges, charge_buf.at[1]),
        (basis, basis_buf),
        (transfers, transfer_buf),
        (pair_coupling, pair_buf.at[0]),
        (dev_coupling, dev_buf),
        (near_blocks.at[0], block_buf.at[0]),
        (near_blocks.at[1], block_buf.at[1]),
        (near_list, s_near_list),
        (near_count, s_near_count),
        (dev_list, s_dev_list),
        (dev_count, s_dev_count),
        (pair_list, s_pair_list),
        (pair_count, s_pair_count),
    ]
    local = [pltpu.make_async_copy(a, b, in_sem.at[i]) for i, (a, b) in enumerate(local)]
    for copy in local[:3]:
        copy.start()
    barrier = pltpu.get_barrier_semaphore()
    for there, core, _, _ in peers:
        pl.semaphore_signal(barrier, inc=1, device_id=(there, core), device_id_type=MESH)
    for copy in local[3:]:
        copy.start()

    for copy in local[:3]:
        copy.wait()
    e = transfer_buf[0]
    e01 = e[0:2].reshape(128, 64)
    e012 = dot3(e01, e[2])
    up_high, up_low = halves(jnp.concatenate([e012, e012, e01, e01], axis=1))
    own_charges = charge_buf[1].astype(F32).reshape(16, 256).astype(BF16)
    products = dot(own_charges, basis_buf[...].reshape(128, 256), NT)
    lane = lax.broadcasted_iota(jnp.int32, (8, 128), 1)
    row = lax.broadcasted_iota(jnp.int32, (8, 128), 0)
    leaf_coeff = stacked(jnp.where(lane < 64, products[0:8], products[8:16]))
    raised = folded(dot(leaf_coeff, up_high) + dot(leaf_coeff, up_low))
    lift, coeff = raised[:, 0:128], raised[:, 128:256]
    my_tile = 2 * own + g
    straight = (row < 4) == (lane < 64)
    tiles[my_tile] = jnp.where(
        straight,
        jnp.where(row < 4, lift, coeff),
        pltpu.roll(jnp.where(row < 4, coeff, lift), 4, 0),
    )

    pl.semaphore_wait(barrier, count)
    sends = []
    for there, core, place, whole in peers:
        rows = pl.ds(0, 8 if whole else 4)
        sends.append(
            pltpu.make_async_remote_copy(
                src_ref=tiles.at[my_tile, rows],
                dst_ref=tiles.at[place, rows],
                send_sem=tile_send,
                recv_sem=tile_recv,
                device_id=(there, core),
                device_id_type=MESH,
            )
        )
    beside = (lax.rem(q + side + pairs, pairs), other)
    to_partner = pltpu.make_async_remote_copy(
        src_ref=charges,
        dst_ref=charge_buf.at[2 * g],
        send_sem=charge_send.at[0],
        recv_sem=charge_recv.at[0],
        device_id=(q, other),
        device_id_type=MESH,
    )
    to_beside = pltpu.make_async_remote_copy(
        src_ref=charges,
        dst_ref=charge_buf.at[2 - 2 * g],
        send_sem=charge_send.at[1],
        recv_sem=charge_recv.at[1],
        device_id=beside,
        device_id_type=MESH,
    )
    give_list = pltpu.make_async_remote_copy(
        src_ref=pair_list,
        dst_ref=partner_list,
        send_sem=list_send,
        recv_sem=list_recv,
        device_id=(q, other),
        device_id_type=MESH,
    )
    give_coupling = pltpu.make_async_remote_copy(
        src_ref=pair_coupling,
        dst_ref=pair_buf.at[1],
        send_sem=coupling_send,
        recv_sem=coupling_recv,
        device_id=(q, other),
        device_id_type=MESH,
    )
    others = [to_beside, to_partner, give_coupling, give_list]
    for copy in sends + others:
        copy.start()

    for copy in local[3:5]:
        copy.wait()
    for copy in local[7:]:
        copy.wait()
    e2h, e2l = halves(e[2])

    def through_pair(blocks):
        rows = blocks.reshape(512, 64)
        rh, rl = halves(rows)
        return (dot(rh, e2h, NT) + dot(rl, e2h, NT) + dot(rh, e2l, NT)).reshape(8, 64, 64)

    def used(slot, total):
        return jnp.where(slot < total, 1.0, 0.0).astype(F32)

    dev_total = s_dev_count[0]
    pair_total = s_pair_count[0]
    lifted = through_pair(pair_buf[0, 0])
    for s in range(8):
        w = jnp.concatenate(
            [dev_buf[0, s] * used(s, dev_total), lifted[s] * used(8 * g + s, pair_total)], axis=0
        )
        weights[s] = jnp.concatenate(halves(w), axis=1)

    down = [
        dot(e_part, basis_buf[l], TN)
        for l in range(2)
        for e_part in halves(e[l])
    ]
    down = jnp.concatenate([down[0] + down[1], down[2] + down[3]], axis=1)
    down = jnp.concatenate(halves(down), axis=0)

    for copy in (to_beside, to_partner):
        copy.wait_recv()
    for copy in local[5:7]:
        copy.wait()
    first = 2 * (2 * q + g) - 2
    near = []
    for l in range(2):
        total = jnp.zeros((8, 256), F32)
        for s in range(6):
            at = jnp.clip(s_near_list[l, s] - first, 0, 5)
            picked = charge_buf[at // 2, at % 2].astype(F32) * used(s, s_near_count[l])
            total += dot(picked.astype(BF16), block_buf[l, s])
        near.append(total)

    give_coupling.wait_recv()
    give_list.wait_recv()
    lifted = through_pair(pair_buf[1, 0])
    for t in range(4):
        w = jnp.concatenate(
            [lifted[s] * used(8 * other + s, pair_total) for s in (2 * t + 1, 2 * t)], axis=0
        )
        weights[8 + t] = jnp.concatenate(halves(w), axis=1)

    def place_of(offset, rows):
        near_by = jnp.where(offset <= REACH, offset + REACH, offset - rows + REACH)
        return jnp.clip(jnp.where(offset == half, last, near_by), 0, last)

    dev_at, pair_at, partner_at = [], [], []
    for s in range(8):
        source = s_dev_list[0, s]
        offset = lax.rem(source // 2 - q + pairs, pairs)
        dev_at.append(2 * place_of(offset, pairs) + source % 2)
        pair_at.append(place_of(lax.rem(s_pair_list[0, s] - q + pairs, pairs), pairs))
        partner_at.append(place_of(lax.rem(partner_list[0, s] - q + pairs, pairs), pairs))

    everyone = tiles.at[pl.ds(0, received)]
    pltpu.make_async_copy(everyone, everyone, tile_recv).wait()

    def pair_tile(at):
        return tiles[2 * at] + tiles[2 * at + 1]

    def unpacked(tile):
        return jnp.where(straight, pltpu.roll(tile, 4, 0), pltpu.roll(tile, 64, 1))

    sources = []
    for s in range(8):
        sources.append(unpacked(jnp.where(row < 4, pair_tile(pair_at[s]), tiles[dev_at[s]])))
    for t in range(4):
        first_pair, second_pair = pair_tile(partner_at[2 * t]), pair_tile(partner_at[2 * t + 1])
        sources.append(unpacked(jnp.where(row < 4, first_pair, pltpu.roll(second_pair, 4, 0))))
    sources = stacked(jnp.concatenate(sources, axis=1))
    root = folded(dot(sources, weights[...].reshape(12 * 128, 128)))
    root = stacked(root + pltpu.roll(root, 64, 1))
    far = folded(dot(root, down))
    for l in range(2):
        out[l] = near[l] + far[:, 256 * l : 256 * (l + 1)]

    pltpu.make_async_copy(everyone, everyone, tile_send).wait()
    for copy in others:
        copy.wait_send()


def per_device(*arrays):
    pairs = lax.axis_size("leaf")
    hbm = pl.BlockSpec(memory_space=pl.ANY)
    dma = pltpu.SemaphoreType.DMA
    return pl.pallas_call(
        functools.partial(kernel, pairs),
        out_shape=jax.ShapeDtypeStruct((2, 8, 256), F32),
        in_specs=[hbm] * len(arrays),
        out_specs=pl.BlockSpec(memory_space=pltpu.VMEM),
        scratch_shapes=[
            pltpu.VMEM((3, 2, 8, 256), BF16),
            pltpu.VMEM((2, 64, 256), BF16),
            pltpu.VMEM((1, 3, 64, 64), F32),
            pltpu.VMEM((2, 6, 256, 256), BF16),
            pltpu.VMEM((1, 8, 64, 64), F32),
            pltpu.VMEM((2, 1, 8, 64, 64), F32),
            pltpu.VMEM((24, 8, 128), F32),
            pltpu.VMEM((12, 128, 128), BF16),
            pltpu.SMEM((2, 6), jnp.int32),
            pltpu.SMEM((2,), jnp.int32),
            pltpu.SMEM((1, 8), jnp.int32),
            pltpu.SMEM((1,), jnp.int32),
            pltpu.SMEM((1, 8), jnp.int32),
            pltpu.SMEM((1,), jnp.int32),
            pltpu.SMEM((1, 8), jnp.int32),
            dma((13,)),
            dma,
            dma,
            dma((2,)),
            dma((2,)),
            dma,
            dma,
            dma,
            dma,
        ],
        compiler_params=pltpu.CompilerParams(
            collective_id=0, has_side_effects=True, vmem_limit_bytes=32 * 1024 * 1024
        ),
        name="h2_product",
    )(*[a if a.size == 1 else pltpu.with_memory_space_constraint(a, pltpu.HBM) for a in arrays])


def solution(mesh):
    both = ("leaf", "grp")
    return jax.shard_map(
        per_device,
        mesh=mesh,
        in_specs=(
            P(both, None, None),
            P(both, None, None),
            P(both, None, None, None),
            P(both, None, None, None),
            P(both, None),
            P(both),
            P(both, None, None, None),
            P(both, None),
            P(both),
            P("leaf", "grp", None, None),
            P("leaf", "grp"),
            P("leaf"),
        ),
        out_specs=P(both, None, None),
        check_vma=False,
    )
```

```python
import functools

import jax
import jax.numpy as jnp
from jax import lax
from jax.experimental import pallas as pl
from jax.experimental.pallas import tpu as pltpu
from jax.sharding import PartitionSpec as P

MESH = pl.DeviceIdType.MESH
REACH = 5
F32 = jnp.float32
BF16 = jnp.bfloat16
NN = (((1,), (0,)), ((), ()))
NT = (((1,), (1,)), ((), ()))
TN = (((0,), (0,)), ((), ()))


def dot(a, b, dims=NN):
    return lax.dot_general(a, b, dims, preferred_element_type=F32)


def halves(a):
    high = a.astype(BF16)
    return high, (a - high.astype(F32)).astype(BF16)


def dot3(a, b, dims=NN):
    ah, al = halves(a)
    bh, bl = halves(b)
    return dot(ah, bh, dims) + dot(al, bh, dims) + dot(ah, bl, dims)


def stacked(a):
    high = a.astype(BF16).astype(F32)
    return jnp.concatenate([high, a - high], axis=0).astype(BF16)


def folded(a):
    return a[0:8] + a[8:16]


def wrapped(at, rows):
    at = jnp.where(at < 0, at + rows, at)
    return jnp.where(at < rows, at, at - rows)


def kernel(
    pairs,
    charges,
    basis,
    transfers,
    near_blocks,
    near_list,
    near_count,
    dev_coupling,
    dev_list,
    dev_count,
    pair_coupling,
    pair_list,
    pair_count,
    out,
    charge_buf,
    basis_buf,
    transfer_buf,
    block_buf,
    dev_buf,
    pair_buf,
    tiles,
    dev_weights,
    pair_weights,
    s_near_list,
    s_near_count,
    s_dev_list,
    s_dev_count,
    s_pair_list,
    s_pair_count,
    partner_list,
    in_sem,
    tile_send,
    tile_recv,
    charge_send,
    charge_recv,
    coupling_send,
    coupling_recv,
    list_send,
    list_recv,
):
    q = lax.axis_index("leaf")
    g = lax.axis_index("grp")
    other = 1 - g
    half = pairs // 2
    own = REACH
    last = 2 * REACH + 1

    side = 2 * g - 1
    peers = []
    for shift, same, cross in (
        (2, True, True),
        (1, True, True),
        (3 * side, False, True),
        (-3 * side, False, False),
        (4, False, False),
        (5, False, False),
        (half, True, False),
        (-1, True, True),
        (-2, True, True),
        (-4, False, False),
        (-5, False, False),
    ):
        there = wrapped(q + shift, pairs)
        place = 2 * (last if shift is half else own - shift) + g
        peers.append((there, g, place, same))
        peers.append((there, other, place, cross))
    peers.append((q, other, 2 * own + g, True))
    count = len(peers)
    whole_tiles = sum(whole for *_, whole in peers)
    received = whole_tiles + (count - whole_tiles) // 2

    local = [
        (charges, charge_buf.at[1]),
        (basis, basis_buf),
        (transfers, transfer_buf),
        (pair_coupling, pair_buf.at[0]),
        (dev_coupling, dev_buf),
        (near_blocks.at[0], block_buf.at[0]),
        (near_blocks.at[1], block_buf.at[1]),
        (near_list, s_near_list),
        (near_count, s_near_count),
        (dev_list, s_dev_list),
        (dev_count, s_dev_count),
        (pair_list, s_pair_list),
        (pair_count, s_pair_count),
    ]
    local = [pltpu.make_async_copy(a, b, in_sem.at[i]) for i, (a, b) in enumerate(local)]
    for copy in local[:3]:
        copy.start()
    barrier = pltpu.get_barrier_semaphore()
    for there, core, _, _ in peers:
        pl.semaphore_signal(barrier, inc=1, device_id=(there, core), device_id_type=MESH)
    for copy in local[3:]:
        copy.start()

    for copy in local[:3]:
        copy.wait()
    e = transfer_buf[0]
    e01 = e[0:2].reshape(128, 64)
    e012 = dot3(e01, e[2])
    up_high, up_low = halves(jnp.concatenate([e012, e012, e01, e01], axis=1))
    own_charges = charge_buf[1].astype(F32).reshape(16, 256).astype(BF16)
    products = dot(own_charges, basis_buf[...].reshape(128, 256), NT)
    lane = lax.broadcasted_iota(jnp.int32, (8, 128), 1)
    row = lax.broadcasted_iota(jnp.int32, (8, 128), 0)
    leaf_coeff = stacked(jnp.where(lane < 64, products[0:8], products[8:16]))
    raised = folded(dot(leaf_coeff, up_high) + dot(leaf_coeff, up_low))
    lift, coeff = raised[:, 0:128], raised[:, 128:256]
    my_tile = 2 * own + g
    straight = (row < 4) == (lane < 64)
    tiles[my_tile] = jnp.where(
        straight,
        jnp.where(row < 4, lift, coeff),
        pltpu.roll(jnp.where(row < 4, coeff, lift), 4, 0),
    )

    pl.semaphore_wait(barrier, count)
    sends = []
    for there, core, place, whole in peers:
        rows = pl.ds(0, 8 if whole else 4)
        sends.append(
            pltpu.make_async_remote_copy(
                src_ref=tiles.at[my_tile, rows],
                dst_ref=tiles.at[place, rows],
                send_sem=tile_send,
                recv_sem=tile_recv,
                device_id=(there, core),
                device_id_type=MESH,
            )
        )
    beside = (wrapped(q + side, pairs), other)
    to_partner = pltpu.make_async_remote_copy(
        src_ref=charges,
        dst_ref=charge_buf.at[2 * g],
        send_sem=charge_send.at[0],
        recv_sem=charge_recv.at[0],
        device_id=(q, other),
        device_id_type=MESH,
    )
    to_beside = pltpu.make_async_remote_copy(
        src_ref=charges,
        dst_ref=charge_buf.at[2 - 2 * g],
        send_sem=charge_send.at[1],
        recv_sem=charge_recv.at[1],
        device_id=beside,
        device_id_type=MESH,
    )
    give_list = pltpu.make_async_remote_copy(
        src_ref=pair_list,
        dst_ref=partner_list,
        send_sem=list_send,
        recv_sem=list_recv,
        device_id=(q, other),
        device_id_type=MESH,
    )
    give_coupling = pltpu.make_async_remote_copy(
        src_ref=pair_coupling,
        dst_ref=pair_buf.at[1],
        send_sem=coupling_send,
        recv_sem=coupling_recv,
        device_id=(q, other),
        device_id_type=MESH,
    )
    others = [to_beside, to_partner, give_coupling, give_list]
    for copy in others[:2] + sends[:8] + others[2:] + sends[8:]:
        copy.start()

    for copy in local[3:5]:
        copy.wait()
    for copy in local[7:]:
        copy.wait()

    def used(slot, total):
        return jnp.where(slot < total, 1.0, 0.0).astype(F32)

    def weigh(coupling, slot, total):
        return jnp.concatenate(halves(coupling * used(slot, total)), axis=1)

    dev_total = s_dev_count[0]
    pair_total = s_pair_count[0]
    for s in range(8):
        dev_weights[s] = weigh(dev_buf[0, s], s, dev_total)
        pair_weights[s] = weigh(pair_buf[0, 0, s], 8 * g + s, pair_total)

    down = []
    for l in range(2):
        high, low = halves(e[l])
        down.append(dot(high, basis_buf[l], TN) + dot(low, basis_buf[l], TN))
    down = jnp.concatenate(down, axis=1)
    down = jnp.concatenate([down, dot3(e[2], down, TN)], axis=0)
    down = jnp.concatenate(halves(down), axis=0)

    for copy in (to_beside, to_partner):
        copy.wait_recv()
    for copy in local[5:7]:
        copy.wait()
    lowest = 2 * (2 * q + g) - 2
    near = []
    for l in range(2):
        total = jnp.zeros((8, 256), F32)
        for s in range(6):
            at = jnp.clip(s_near_list[l, s] - lowest, 0, 5)
            picked = charge_buf[at // 2, at % 2].astype(F32) * used(s, s_near_count[l])
            total += dot(picked.astype(BF16), block_buf[l, s])
        near.append(total)

    give_coupling.wait_recv()
    give_list.wait_recv()
    for s in range(8):
        pair_weights[8 + s] = weigh(pair_buf[1, 0, s], 8 * other + s, pair_total)

    def place_of(source):
        offset = source - q
        offset = jnp.where(offset > half, offset - pairs, jnp.where(offset < -half, offset + pairs, offset))
        return jnp.clip(jnp.where(jnp.abs(offset) == half, last, offset + own), 0, last)

    dev_at = []
    for s in range(8):
        source = s_dev_list[0, s]
        dev_at.append(2 * place_of(source >> 1) + (source & 1))
    pair_at = [place_of(ref[0, s]) for ref in (s_pair_list, partner_list) for s in range(8)]

    everyone = tiles.at[pl.ds(0, received)]
    pltpu.make_async_copy(everyone, everyone, tile_recv).wait()

    def pair_tile(at):
        return tiles[2 * at] + tiles[2 * at + 1]

    def unpacked(tile):
        return jnp.where(straight, pltpu.roll(tile, 4, 0), pltpu.roll(tile, 64, 1))

    dev_sources, pair_sources = [], []
    for t in range(0, 8, 2):
        first, second = (tiles[dev_at[s]] for s in (t, t + 1))
        dev_sources.append(unpacked(jnp.where(row < 4, pltpu.roll(second, 4, 0), first)))
    for t in range(0, 16, 2):
        first, second = (pair_tile(pair_at[s]) for s in (t, t + 1))
        pair_sources.append(unpacked(jnp.where(row < 4, second, pltpu.roll(first, 4, 0))))

    def gathered(sources, weights, slots):
        sources = stacked(jnp.concatenate(sources, axis=1))
        sums = folded(dot(sources, weights[...].reshape(slots * 64, 128)))
        return sums + pltpu.roll(sums, 64, 1)

    field = jnp.where(
        lane < 64, gathered(dev_sources, dev_weights, 8), gathered(pair_sources, pair_weights, 16)
    )
    field = stacked(field)
    far = folded(dot(jnp.concatenate([field, field], axis=1), down))
    for l in range(2):
        out[l] = near[l] + far[:, 256 * l : 256 * (l + 1)]

    pltpu.make_async_copy(everyone, everyone, tile_send).wait()
    for copy in others:
        copy.wait_send()


def per_device(*arrays):
    pairs = lax.axis_size("leaf")
    hbm = pl.BlockSpec(memory_space=pl.ANY)
    dma = pltpu.SemaphoreType.DMA
    return pl.pallas_call(
        functools.partial(kernel, pairs),
        out_shape=jax.ShapeDtypeStruct((2, 8, 256), F32),
        in_specs=[hbm] * len(arrays),
        out_specs=pl.BlockSpec(memory_space=pltpu.VMEM),
        scratch_shapes=[
            pltpu.VMEM((3, 2, 8, 256), BF16),
            pltpu.VMEM((2, 64, 256), BF16),
            pltpu.VMEM((1, 3, 64, 64), F32),
            pltpu.VMEM((2, 6, 256, 256), BF16),
            pltpu.VMEM((1, 8, 64, 64), F32),
            pltpu.VMEM((2, 1, 8, 64, 64), F32),
            pltpu.VMEM((24, 8, 128), F32),
            pltpu.VMEM((8, 64, 128), BF16),
            pltpu.VMEM((16, 64, 128), BF16),
            pltpu.SMEM((2, 6), jnp.int32),
            pltpu.SMEM((2,), jnp.int32),
            pltpu.SMEM((1, 8), jnp.int32),
            pltpu.SMEM((1,), jnp.int32),
            pltpu.SMEM((1, 8), jnp.int32),
            pltpu.SMEM((1,), jnp.int32),
            pltpu.SMEM((1, 8), jnp.int32),
            dma((13,)),
            dma,
            dma,
            dma((2,)),
            dma((2,)),
            dma,
            dma,
            dma,
            dma,
        ],
        compiler_params=pltpu.CompilerParams(
            collective_id=0, has_side_effects=True, vmem_limit_bytes=32 * 1024 * 1024
        ),
        name="h2_product",
    )(*[a if a.size == 1 else pltpu.with_memory_space_constraint(a, pltpu.HBM) for a in arrays])


def solution(mesh):
    both = ("leaf", "grp")
    return jax.shard_map(
        per_device,
        mesh=mesh,
        in_specs=(
            P(both, None, None),
            P(both, None, None),
            P(both, None, None, None),
            P(both, None, None, None),
            P(both, None),
            P(both),
            P(both, None, None, None),
            P(both, None),
            P(both),
            P("leaf", "grp", None, None),
            P("leaf", "grp"),
            P("leaf"),
        ),
        out_specs=P(both, None, None),
        check_vma=False,
    )
```
